128 devices in a mesh: region: 16 (over z, x), sub: 8 (over y, core).
Axes of the slice: x: 4, y: 4, z: 4, core: 2. Of those that a mesh axis runs over, the one named last changes fastest.
Arguments:
- nodes: bfloat16 [65536, 512], P(('region', 'sub')), may hold values from -6 to 6
- edges: bfloat16 [393216, 512], P(('region', 'sub')), may hold values from -6 to 6
- sender: int32 [393216], P(('region', 'sub')), may hold values from 0 to 1247, as said below
- receiver: int32 [393216], P(('region', 'sub')), may hold values from 0 to 511, as said below
- tile_counts: int32 [1536], P(('region', 'sub')), may hold values from 64 to 256, as said below
- send_list: int32 [128, 736], P(('region', 'sub')), may hold values from 0 to 511, as said below
- edge_w1: bfloat16 [1536, 512], replicated, may hold values from -0.15625 to 0.15625
- edge_w2: bfloat16 [512, 512], replicated, may hold values from -0.25 to 0.25
- edge_gain: float32 [512], replicated, may hold values from 0.5 to 1.5
- node_w1: bfloat16 [1024, 512], replicated, may hold values from -0.1875 to 0.1875
- node_w2: bfloat16 [512, 512], replicated, may hold values from -0.25 to 0.25
- node_gain: float32 [512], replicated, may hold values from 0.5 to 1.5
- node_cotangent: bfloat16 [65536, 512], P(('region', 'sub')), may hold values from -6 to 6
- edge_cotangent: bfloat16 [393216, 512], P(('region', 'sub')), may hold values from -6 to 6
Outputs:
- edge_out: bfloat16 [393216, 512], P(('region', 'sub'))
- node_out: bfloat16 [65536, 512], P(('region', 'sub'))
- grad_edges: bfloat16 [393216, 512], P(('region', 'sub'))
- grad_nodes: bfloat16 [65536, 512], P(('region', 'sub'))
The draws below stay inside these ranges and needn't reach their ends.
Inputs may be any that keep to these rules, and one draw needn't show every extreme that they name: `sender`: below 512: a node of the edge's own block b. 512 + o * 80 + s for o below 6: slot s of the rows that block b - d_o (modulo the number of blocks; d = 1, 2, 3, -1, -2, -3) sends to block b. 512 + 6 * 80 + p * 2 + s: slot s of the rows that block p sends to block b. Each value from 512 upward is taken by exactly one live edge of each block. `receiver`: Non-decreasing within each block of 3072 edges; 0 and 511 occur in every block. `tile_counts`: every block has a full tile. `send_list`: row b: positions o * 80 to o * 80 + 79, local nodes of block b sent to block b + d_o (modulo the number of blocks); positions 480 + p * 2 to 480 + p * 2 + 1, local nodes of block b sent to block p; a node may appear several times.
All inputs are finite; a program needn't handle non-finite values.
Results may differ from the reference program's by a relative error of at most 0.015.
Values may be sent and summed in bfloat16 or wider, within the bound.
No kernel may reach another device: no remote copies, remote signals or barrier semaphores. Data moves between devices by JAX's collectives and lax.ppermute only.
A program may use at most 192 MiB of HBM per device.

```python
import jax
import jax.numpy as jnp
from jax import lax

D = 512
NODE_DEV = 512
TILES_DEV = 12
TILE = 256
NEAR_SLOTS = 80
FAR_SLOTS = 2
NODES = 65536
EDGES = 393216
N_REGION = 16
N_SUB = 8


def force_value(key, values, target):
    position = jax.random.randint(key, (values.shape[0], 1), 0, values.shape[1])
    column = lax.broadcasted_iota(jnp.int32, values.shape, 1)
    return jnp.where(column == position, target, values)


def tile_table(key):
    key = jax.random.fold_in(key, 37)
    first, second = jax.random.split(key, 2)
    blocks_all = N_REGION * N_SUB
    values = jax.random.randint(first, (blocks_all, TILES_DEV), TILE // 4, TILE + 1)
    return force_value(second, values, TILE).astype(jnp.int32)


def shuffle_row(key, count):
    return jax.random.permutation(key, count).astype(jnp.int32)


def draw_tile_counts(key, part):
    counts = tile_table(key)
    return counts.reshape(-1).astype(jnp.int32)


def draw_sender(key, part):
    counts = tile_table(key)
    key = jax.random.fold_in(key, 11)
    first, second = jax.random.split(key, 2)
    blocks_all = N_REGION * N_SUB
    count = TILES_DEV * TILE
    forced = 6 * NEAR_SLOTS + blocks_all * FAR_SLOTS
    position = lax.broadcasted_iota(jnp.int32, (blocks_all, TILES_DEV, TILE), 2)
    dead = (position >= counts[:, :, None]).astype(jnp.int32).reshape(blocks_all, count)
    shuffled = jax.vmap(partial_shuffle(count))(jax.random.split(second, blocks_all))
    score = shuffled + count * dead
    ordering = jnp.argsort(score, axis=1, stable=True)
    rank = jnp.argsort(ordering, axis=1, stable=True).astype(jnp.int32)
    nearby = jax.random.randint(first, (blocks_all, count), 0, NODE_DEV)
    values = jnp.where(rank < forced, NODE_DEV + rank, nearby)
    return values.reshape(-1).astype(jnp.int32)


def partial_shuffle(count):

    def shuffle_one(key):
        return shuffle_row(key, count)
    return shuffle_one


def draw_receiver(key, part):
    key = jax.random.fold_in(key, 23)
    first, second = jax.random.split(key, 2)
    blocks_all = N_REGION * N_SUB
    count = TILES_DEV * TILE
    values = jax.random.randint(first, (blocks_all, count), 0, NODE_DEV)
    position = jax.random.randint(second, (blocks_all, 1), 0, count)
    column = lax.broadcasted_iota(jnp.int32, values.shape, 1)
    values = jnp.where(column == position, NODE_DEV - 1, values)
    values = jnp.where(column == (position + 1) % count, 0, values)
    return jnp.sort(values, axis=1).reshape(-1).astype(jnp.int32)


def draw_send_list(key, part):
    key = jax.random.fold_in(key, 41)
    first, second = jax.random.split(key, 2)
    blocks_all = N_REGION * N_SUB
    columns = 6 * NEAR_SLOTS + blocks_all * FAR_SLOTS
    values = jax.random.randint(first, (blocks_all, columns), 0, NODE_DEV)
    values = force_value(second, values, NODE_DEV - 1)
    return values.astype(jnp.int32)


def levels(own_key, dims, pieces, smallest, largest):
    def one(axis_at, blocks):
        heights = jax.random.uniform(jax.random.fold_in(jax.random.fold_in(own_key, 6), axis_at), (blocks,), jnp.float32, smallest / len(pieces), largest / len(pieces))
        return jnp.repeat(jnp.exp(heights), dims[axis_at] // blocks).reshape((-1,) + (1,) * (len(dims) - axis_at - 1))

    level = one(*pieces[0])
    for cut in pieces[1:]:
        level = level * one(*cut)
    return level


def scatter_about(own_key, extent, scale, most, pieces=(), kind=jnp.bfloat16):
    values = scale * jax.random.normal(own_key, extent, jnp.float32)
    if pieces:
        values = values * levels(own_key, extent, pieces, -0.22, 0.18)
    return jnp.clip(values, -most, most).astype(kind)


def setup_inputs(seed: int = 0) -> dict:
    streams_of = jax.random.split(jax.random.key(seed), 15)
    nodes = scatter_about(streams_of[0], (NODES, D), 1.0, 6.0, ((0, 128),))
    edges = scatter_about(streams_of[1], (EDGES, D), 1.0, 6.0, ((0, 128),))
    sender = draw_sender(jax.random.fold_in(streams_of[14], 71), 0)
    receiver = draw_receiver(jax.random.fold_in(streams_of[14], 71), 0)
    tile_counts = draw_tile_counts(jax.random.fold_in(streams_of[14], 71), 0)
    send_list = draw_send_list(jax.random.fold_in(streams_of[14], 71), 0)
    edge_w1 = scatter_about(streams_of[6], (3 * D, D), (3 * D) ** -0.5, 0.15625)
    edge_w2 = scatter_about(streams_of[7], (D, D), D ** -0.5, 0.25)
    edge_gain = jnp.clip(1.0 + 0.1 * jax.random.normal(streams_of[8], (D,), jnp.float32), 0.5, 1.5)
    node_w1 = scatter_about(streams_of[9], (2 * D, D), (2 * D) ** -0.5, 0.1875)
    node_w2 = scatter_about(streams_of[10], (D, D), D ** -0.5, 0.25)
    node_gain = jnp.clip(1.0 + 0.1 * jax.random.normal(streams_of[11], (D,), jnp.float32), 0.5, 1.5)
    node_cotangent = scatter_about(streams_of[12], (NODES, D), 1.0, 6.0, ((0, 128),))
    edge_cotangent = scatter_about(streams_of[13], (EDGES, D), 1.0, 6.0, ((0, 128),))
    return {"nodes": nodes, "edges": edges, "sender": sender, "receiver": receiver, "tile_counts": tile_counts, "send_list": send_list, "edge_w1": edge_w1, "edge_w2": edge_w2, "edge_gain": edge_gain, "node_w1": node_w1, "node_w2": node_w2, "node_gain": node_gain, "node_cotangent": node_cotangent, "edge_cotangent": edge_cotangent}


def layer_norm(mixed, gain):
    centre = mixed - lax.optimization_barrier(jnp.mean(mixed, axis=-1, keepdims=True))
    spread = lax.rsqrt(lax.optimization_barrier(jnp.mean(centre * centre, axis=-1, keepdims=True)) + 1e-05)
    normal = centre * spread
    return (normal * gain, normal, spread)

def norm_back(upper, gain, normal, spread):
    scaled = upper * gain
    return spread * (scaled - lax.optimization_barrier(jnp.mean(scaled, axis=-1, keepdims=True)) - normal * lax.optimization_barrier(jnp.mean(scaled * normal, axis=-1, keepdims=True)))

def silu_slope(hidden):
    sigma = jax.nn.sigmoid(hidden)
    return sigma * (1.0 + hidden * (1.0 - sigma))

def back_dot(left, weight):
    return lax.dot_general(left, weight, (((1,), (1,)), ((), ())), preferred_element_type=jnp.float32)

def edge_forward(edge_rows, from_rows, to_rows, mask_rows, first, second, gain):
    joined = jnp.concatenate([edge_rows, from_rows, to_rows], axis=1)
    hidden = jnp.dot(joined, first, preferred_element_type=jnp.float32)
    active = jax.nn.silu(hidden).astype(jnp.bfloat16)
    mixed = jnp.dot(active, second, preferred_element_type=jnp.float32)
    normed, normal, spread = layer_norm(mixed, gain)
    return (hidden, normed * mask_rows[:, None], normal, spread)

def mlp_back(upper, hidden, normal, spread, gain, first, second):
    mixed_grad = norm_back(upper, gain, normal, spread).astype(jnp.bfloat16)
    active_grad = back_dot(mixed_grad, second)
    hidden_grad = (active_grad * silu_slope(hidden)).astype(jnp.bfloat16)
    return back_dot(hidden_grad, first)

def reference(nodes, edges, sender, receiver, tile_counts, send_list, edge_w1, edge_w2, edge_gain, node_w1, node_w2, node_gain, node_cotangent, edge_cotangent):
    blocks_all = N_REGION * N_SUB
    near_total = 6 * NEAR_SLOTS
    blocks = jnp.arange(blocks_all, dtype=jnp.int32)[:, None]
    from_local = sender.reshape(blocks_all, -1)
    to_local = receiver.reshape(blocks_all, -1)
    remote = jnp.maximum(from_local - NODE_DEV, 0).astype(jnp.int32)
    neighbour = jnp.minimum(remote // NEAR_SLOTS, 5).astype(jnp.int32)
    offset = jnp.where(neighbour < 3, neighbour + 1, 2 - neighbour).astype(jnp.int32)
    far_index = jnp.maximum(remote - near_total, 0).astype(jnp.int32)
    is_near = remote < near_total
    source = jnp.where(is_near, (blocks - offset) % blocks_all, far_index // FAR_SLOTS).astype(jnp.int32)
    column = jnp.where(is_near, remote, near_total + blocks * FAR_SLOTS + far_index % FAR_SLOTS).astype(jnp.int32)
    picked = send_list[source, column]
    from_global = jnp.where(from_local < NODE_DEV, blocks * NODE_DEV + from_local, source * NODE_DEV + picked).astype(jnp.int32)
    to_global = (blocks * NODE_DEV + to_local).astype(jnp.int32)
    position = lax.broadcasted_iota(jnp.int32, (blocks_all, TILES_DEV, TILE), 2)
    mask = (position < tile_counts.reshape(blocks_all, TILES_DEV, 1)).astype(jnp.float32).reshape(blocks_all, -1)
    edge_blocks = edges.reshape(blocks_all, -1, D)
    cot_blocks = edge_cotangent.reshape(blocks_all, -1, D)

    def forward_block(item):
        edge_rows, from_ids, to_ids, to_slots, mask_rows = item
        hidden, message, normal, spread = edge_forward(edge_rows, jnp.take(nodes, from_ids, axis=0), jnp.take(nodes, to_ids, axis=0), mask_rows, edge_w1, edge_w2, edge_gain)
        updated = (edge_rows.astype(jnp.float32) + message).astype(jnp.bfloat16)
        summed = jax.ops.segment_sum(message, to_slots, num_segments=NODE_DEV).astype(jnp.bfloat16)
        return (updated, summed, hidden, normal, spread)
    edge_out, aggregate, edge_hidden, edge_normal, edge_spread = lax.map(forward_block, (edge_blocks, from_global, to_global, to_local, mask))
    aggregate = aggregate.reshape(-1, D)
    node_hidden = jnp.dot(jnp.concatenate([nodes, aggregate], axis=1), node_w1, preferred_element_type=jnp.float32)
    node_active = jax.nn.silu(node_hidden).astype(jnp.bfloat16)
    node_mixed = jnp.dot(node_active, node_w2, preferred_element_type=jnp.float32)
    normed, normal, spread = layer_norm(node_mixed, node_gain)
    node_out = (nodes.astype(jnp.float32) + normed).astype(jnp.bfloat16)
    node_cot = node_cotangent.astype(jnp.float32)
    node_input_grad = mlp_back(node_cot, node_hidden, normal, spread, node_gain, node_w1, node_w2)
    direct = node_cot + node_input_grad[:, :D]
    aggregate_grad = node_input_grad[:, D:]

    def backward_block(total, item):
        cot_rows, from_ids, to_ids, mask_rows, hidden, block_normal, block_spread = item
        cot_float = cot_rows.astype(jnp.float32)
        upper = (cot_float + jnp.take(aggregate_grad, to_ids, axis=0)) * mask_rows[:, None]
        input_grad = mlp_back(upper, hidden, block_normal, block_spread, edge_gain, edge_w1, edge_w2)
        total = total.at[from_ids].add(input_grad[:, D:2 * D])
        total = total.at[to_ids].add(input_grad[:, 2 * D:])
        return (total, (cot_float + input_grad[:, :D]).astype(jnp.bfloat16))
    total, grad_edges = lax.scan(backward_block, direct, (cot_blocks, from_global, to_global, mask, edge_hidden, edge_normal, edge_spread))
    return (edge_out.reshape(-1, D), node_out, grad_edges.reshape(-1, D), total.astype(jnp.bfloat16))
```

```python
import functools

import jax
import jax.numpy as jnp
from jax import lax
from jax.experimental import pallas as pl
from jax.experimental.pallas import tpu as pltpu
from jax.sharding import PartitionSpec as P

NEAR = 80
NEAR_TOTAL = 480
TILE = 256
BF = jnp.bfloat16
F32 = jnp.float32
AXES = ("region", "sub")
VMEM = pltpu.VMEM
MIB = 1024 * 1024


def near_offset(neighbour):
    return neighbour + 1 if neighbour < 3 else 2 - neighbour


def shifted(value, steps):
    count = lax.axis_size(AXES)
    return lax.ppermute(value, AXES, [(s, (s + steps) % count) for s in range(count)])


def exchange_far(rows):
    return lax.all_to_all(rows, AXES, split_axis=0, concat_axis=0, tiled=True)


def dot(a, b):
    return lax.dot_general(a, b, (((1,), (0,)), ((), ())), preferred_element_type=F32)


def dot_nt(a, b):
    return lax.dot_general(a, b, (((1,), (1,)), ((), ())), preferred_element_type=F32)


def dot_tn(a, b):
    return lax.dot_general(a, b, (((0,), (0,)), ((), ())), preferred_element_type=F32)


def hot_rows(index_row, first, count):
    ids = lax.broadcasted_iota(jnp.int32, (count, index_row.shape[1]), 0) + first
    return jnp.where(ids == index_row, 1.0, 0.0).astype(BF)


def hot_columns(index_lanes, first, count):
    lane = lax.broadcasted_iota(jnp.int32, index_lanes.shape, 1) + first
    parts = [
        jnp.where(index_lanes == lane + 128 * k, 1.0, 0.0).astype(BF) for k in range(count // 128)
    ]
    return jnp.concatenate(parts, axis=1)


def spread_lanes(index_ref, lanes_ref):
    flipped = jnp.transpose(index_ref[...], (1, 0))
    for j in range(index_ref.shape[0]):
        lanes_ref[pl.ds(j * 128, 128), :] = jnp.broadcast_to(flipped[:, j : j + 1], (128, 128))


def row_mean(x):
    return jnp.sum(x, axis=1, keepdims=True) * (1.0 / x.shape[1])


def normalise(mixed):
    centre = mixed - row_mean(mixed)
    spread = lax.rsqrt(row_mean(centre * centre) + 1e-05)
    return centre * spread, spread


def norm_back(scaled, normal, spread):
    return spread * (scaled - row_mean(scaled) - normal * row_mean(scaled * normal))


def sigmoid(x):
    return 1.0 / (1.0 + jnp.exp(-x))


def slope_of(hidden, sigma):
    return sigma * (1.0 + hidden * (1.0 - sigma))


def tile_rows(t):
    return pl.ds(pl.multiple_of(t * TILE, TILE), TILE)


def copies_of(tiles, src, dst, sems):
    return [
        pltpu.make_async_copy(src.at[tile_rows(t)], dst.at[tile_rows(t)], sems.at[t])
        for t in range(tiles)
    ]


def copy_of(t, src, dst, sems):
    return pltpu.make_async_copy(src.at[tile_rows(t)], dst.at[tile_rows(t)], sems.at[t])


def gather_kernel(nodes_ref, list_ref, *outs):
    hot = hot_rows(list_ref[...], 0, nodes_ref.shape[0])
    rows = dot_tn(hot, nodes_ref[...]).astype(BF)
    for i in range(6):
        outs[i][...] = rows[i * NEAR : (i + 1) * NEAR]
    outs[6][...] = rows[NEAR_TOTAL:]


def local_kernel(
    nodes_ref, sender_ref, receiver_ref, w1_ref, edges_hbm, part_hbm,
    edges, part, slanes, rlanes, table, in_sem, out_sem,
):
    tiles = edges.shape[0] // TILE
    width = nodes_ref.shape[1]
    count = nodes_ref.shape[0]
    for c in copies_of(tiles, edges_hbm, edges, in_sem):
        c.start()
    spread_lanes(sender_ref, slanes)
    spread_lanes(receiver_ref, rlanes)
    nodes = nodes_ref[...]
    table[:count, :] = dot(nodes, w1_ref[width : 2 * width, :]).astype(BF)
    table[count:, :] = dot(nodes, w1_ref[2 * width :, :]).astype(BF)

    def body(t, carry):
        rows = tile_rows(t)
        hot = jnp.concatenate(
            [hot_columns(slanes[rows, :], 0, count), hot_columns(rlanes[rows, :], 0, count)], axis=1
        )
        total = dot(hot, table[...])
        copy_of(t, edges_hbm, edges, in_sem).wait()
        total = total + dot(edges[rows, :], w1_ref[:width, :])
        part[rows, :] = total.astype(BF)
        copy_of(t, part, part_hbm, out_sem).start()
        return carry

    lax.fori_loop(0, tiles, body, 0)
    for c in copies_of(tiles, part, part_hbm, out_sem):
        c.wait()


def main_kernel(
    counts_ref, n0, n1, n2, n3, n4, n5, far_ref, sender_ref, receiver_ref, srow_ref, rrow_ref,
    w1s_ref, w2_ref, gain_ref, nw1_ref, nw2_ref, ngain_ref, nodes_ref, ncot_ref,
    part_hbm, edges_hbm, cot_hbm,
    edge_out_hbm, node_out_ref, hgrad_hbm, r0, r1, r2, r3, r4, r5, rfar, direct_ref,
    part, edges, cot, normals, slopes, hgrad, slanes, rlanes, spreads, table, sums, aggregate,
    agrad, part_sem, edges_sem, cot_sem, eout_sem, hgrad_sem,
):
    tiles = edges.shape[0] // TILE
    count, width = nodes_ref.shape
    halo = table.shape[0]
    for t in range(tiles):
        copy_of(t, part_hbm, part, part_sem).start()
        copy_of(t, edges_hbm, edges, edges_sem).start()
    for c in copies_of(tiles, cot_hbm, cot, cot_sem):
        c.start()
    spread_lanes(sender_ref, slanes)
    spread_lanes(receiver_ref, rlanes)
    arrived = jnp.concatenate([r[...] for r in (n0, n1, n2, n3, n4, n5)] + [far_ref[...]], axis=0)
    table[: arrived.shape[0], :] = dot(arrived, w1s_ref[...]).astype(BF)
    table[arrived.shape[0] :, :] = jnp.zeros((halo - arrived.shape[0], width), BF)
    aggregate[...] = jnp.zeros_like(aggregate)
    sums[...] = jnp.zeros_like(sums)
    gain = gain_ref[...]
    position = lax.broadcasted_iota(jnp.int32, (TILE, 1), 0)

    def forward(t, carry):
        rows = tile_rows(t)
        hot = hot_columns(slanes[rows, :], count, halo)
        remote = dot(hot, table[...])
        copy_of(t, part_hbm, part, part_sem).wait()
        hidden = part[rows, :].astype(F32) + remote
        sigma = sigmoid(hidden)
        slopes[rows, :] = slope_of(hidden, sigma).astype(BF)
        mixed = dot((hidden * sigma).astype(BF), w2_ref[...])
        normal, spread = normalise(mixed)
        normals[rows, :] = normal.astype(BF)
        spreads[rows, :] = spread
        live = (position < counts_ref[t]).astype(F32)
        message = normal * gain * live
        copy_of(t, edges_hbm, edges, edges_sem).wait()
        edges[rows, :] = (edges[rows, :].astype(F32) + message).astype(BF)
        copy_of(t, edges, edge_out_hbm, eout_sem).start()
        into = hot_rows(rrow_ref[t], 0, count)
        aggregate[...] += dot(into, message.astype(BF))
        return carry

    lax.fori_loop(0, tiles, forward, 0)

    nodes = nodes_ref[...]
    node_hidden = dot(nodes, nw1_ref[:width, :]) + dot(aggregate[...].astype(BF), nw1_ref[width:, :])
    sigma = sigmoid(node_hidden)
    node_slope = slope_of(node_hidden, sigma)
    node_mixed = dot((node_hidden * sigma).astype(BF), nw2_ref[...])
    normal, spread = normalise(node_mixed)
    node_out_ref[...] = (nodes.astype(F32) + normal * ngain_ref[...]).astype(BF)
    node_cot = ncot_ref[...].astype(F32)
    mixed_grad = norm_back(node_cot * ngain_ref[...], normal, spread).astype(BF)
    hidden_grad = (dot_nt(mixed_grad, nw2_ref[...]) * node_slope).astype(BF)
    direct_ref[...] = node_cot + dot_nt(hidden_grad, nw1_ref[:width, :])
    agrad[...] = dot_nt(hidden_grad, nw1_ref[width:, :]).astype(BF)

    def backward(t, carry):
        rows = tile_rows(t)
        upper = dot(hot_columns(rlanes[rows, :], 0, count), agrad[...])
        copy_of(t, cot_hbm, cot, cot_sem).wait()
        live = (position < counts_ref[t]).astype(F32)
        scaled = (upper + cot[rows, :].astype(F32)) * gain * live
        grad = norm_back(scaled, normals[rows, :].astype(F32), spreads[rows, :]).astype(BF)
        hg = (dot_nt(grad, w2_ref[...]) * slopes[rows, :].astype(F32)).astype(BF)
        hgrad[rows, :] = hg
        copy_of(t, hgrad, hgrad_hbm, hgrad_sem).start()
        sums[...] += dot(hot_rows(srow_ref[t], count, halo), hg)
        return carry

    lax.fori_loop(0, tiles, backward, 0)
    back = dot_nt(sums[...].astype(BF), w1s_ref[...]).astype(BF)
    for i, ref in enumerate((r0, r1, r2, r3, r4, r5)):
        ref[...] = back[i * NEAR : (i + 1) * NEAR]
    rfar[...] = back[NEAR_TOTAL : NEAR_TOTAL + rfar.shape[0]]
    for c in copies_of(tiles, edges, edge_out_hbm, eout_sem):
        c.wait()
    for c in copies_of(tiles, hgrad, hgrad_hbm, hgrad_sem):
        c.wait()


def rest_kernel(
    srow_ref, rrow_ref, w1_ref, direct_ref, hgrad_hbm, cot_hbm, grad_hbm, owned_ref,
    hgrad, cot, sums, h_sem, c_sem, out_sem,
):
    tiles = hgrad.shape[0] // TILE
    count, width = direct_ref.shape
    for t in range(tiles):
        copy_of(t, hgrad_hbm, hgrad, h_sem).start()
        copy_of(t, cot_hbm, cot, c_sem).start()
    sums[...] = jnp.zeros_like(sums)

    def body(t, carry):
        rows = tile_rows(t)
        copy_of(t, hgrad_hbm, hgrad, h_sem).wait()
        copy_of(t, cot_hbm, cot, c_sem).wait()
        hg = hgrad[rows, :]
        cot[rows, :] = (cot[rows, :].astype(F32) + dot_nt(hg, w1_ref[:width, :])).astype(BF)
        copy_of(t, cot, grad_hbm, out_sem).start()
        sums[:count, :] += dot(hot_rows(srow_ref[t], 0, count), hg)
        sums[count:, :] += dot(hot_rows(rrow_ref[t], 0, count), hg)
        return carry

    lax.fori_loop(0, tiles, body, 0)
    owned_ref[...] = (
        direct_ref[...]
        + dot_nt(sums[:count, :].astype(BF), w1_ref[width : 2 * width, :])
        + dot_nt(sums[count:, :].astype(BF), w1_ref[2 * width :, :])
    )
    for c in copies_of(tiles, cot, grad_hbm, out_sem):
        c.wait()


def final_kernel(list_ref, owned_ref, n0, n1, n2, n3, n4, n5, far_ref, out_ref):
    returned = jnp.concatenate([r[...] for r in (n0, n1, n2, n3, n4, n5)] + [far_ref[...]], axis=0)
    hot = hot_rows(list_ref[...], 0, owned_ref.shape[0])
    out_ref[...] = (owned_ref[...] + dot(hot, returned)).astype(BF)


def kernel_call(body, outs, in_specs, out_specs, scratch, flops, moved, limit):
    return pl.pallas_call(
        body,
        out_shape=outs,
        in_specs=in_specs,
        out_specs=out_specs,
        scratch_shapes=scratch,
        compiler_params=pltpu.CompilerParams(vmem_limit_bytes=limit * MIB),
        cost_estimate=pl.CostEstimate(flops=flops, bytes_accessed=moved, transcendentals=0),
    )


def on_device(
    nodes, edges, sender, receiver, tile_counts, send_list, edge_w1, edge_w2, edge_gain,
    node_w1, node_w2, node_gain, node_cotangent, edge_cotangent,
):
    count, width = nodes.shape
    slots = edges.shape[0]
    tiles = slots // TILE
    halo = send_list.shape[1]
    far_rows = halo - NEAR_TOTAL
    padded = -(-halo // 256) * 256
    v = pl.BlockSpec(memory_space=pltpu.VMEM)
    s = pl.BlockSpec(memory_space=pltpu.SMEM)
    a = pl.BlockSpec(memory_space=pl.ANY)
    sds = jax.ShapeDtypeStruct
    sem = pltpu.SemaphoreType.DMA((tiles,))
    near_shapes = [sds((NEAR, width), BF)] * 6 + [sds((far_rows, width), BF)]
    big = sds((slots, width), BF)
    wide = VMEM((slots, width), BF)
    lanes = VMEM((slots, 128), jnp.int32)
    square = 2 * count * width * width

    sender_lanes = sender.reshape(slots // 128, 128)
    receiver_lanes = receiver.reshape(slots // 128, 128)
    sender_rows = sender.reshape(tiles, 1, TILE)
    receiver_rows = receiver.reshape(tiles, 1, TILE)
    gain = edge_gain.reshape(1, width)
    ngain = node_gain.reshape(1, width)

    leaving = kernel_call(
        gather_kernel, near_shapes, [v, v], [v] * 7, [], 2 * halo * count * width, 2 * MIB, 16
    )(nodes, send_list)
    arrived = [shifted(leaving[i], near_offset(i)) for i in range(6)]
    far = exchange_far(leaving[6])

    part = kernel_call(
        local_kernel, big, [v, v, v, v, a], a,
        [wide, wide, lanes, lanes, VMEM((2 * count, width), BF), sem, sem],
        20 * square, 8 * MIB, 24,
    )(nodes, sender_lanes, receiver_lanes, edge_w1, edges)

    outs = kernel_call(
        main_kernel,
        [big, sds((count, width), BF), big] + near_shapes + [sds((count, width), F32)],
        [s] + [v] * 19 + [a] * 3,
        [a, v, a] + [v] * 8,
        [wide] * 6
        + [lanes, lanes, VMEM((slots, 1), F32), VMEM((padded, width), BF), VMEM((padded, width), F32),
           VMEM((count, width), F32), VMEM((count, width), BF)]
        + [sem] * 5,
        50 * square, 20 * MIB, 48,
    )(
        tile_counts, *arrived, far, sender_lanes, receiver_lanes, sender_rows, receiver_rows,
        edge_w1[width : 2 * width], edge_w2, gain, node_w1, node_w2, ngain, nodes, node_cotangent,
        part, edges, edge_cotangent,
    )
    edge_out, node_out, hgrad = outs[:3]
    back = outs[3:10]
    direct = outs[10]
    returned = [shifted(back[i], -near_offset(i)) for i in range(6)]
    far_back = exchange_far(back[6])

    grad_edges, owned = kernel_call(
        rest_kernel, [big, sds((count, width), F32)], [v] * 4 + [a, a], [a, v],
        [wide, wide, VMEM((2 * count, width), F32), sem, sem, sem],
        20 * square, 12 * MIB, 24,
    )(sender_rows, receiver_rows, edge_w1, direct, hgrad, edge_cotangent)

    grad_nodes = kernel_call(
        final_kernel, sds((count, width), BF), [v] * 9, v, [], 2 * square, 3 * MIB, 16
    )(send_list, owned, *returned, far_back)
    return edge_out, node_out, grad_edges, grad_nodes


def solution(mesh):
    rows = P(AXES, None)
    flat = P(AXES)
    in_specs = (
        rows, rows, flat, flat, flat, rows, P(), P(), P(), P(), P(), P(), rows, rows,
    )
    return jax.shard_map(
        on_device, mesh=mesh, in_specs=in_specs, out_specs=(rows,) * 4, check_vma=False
    )
```

```python
import functools

import jax
import jax.numpy as jnp
from jax import lax
from jax.experimental import pallas as pl
from jax.experimental.pallas import tpu as pltpu
from jax.sharding import PartitionSpec as P

NEAR = 80
NEAR_TOTAL = 480
TILE = 256
BF = jnp.bfloat16
F32 = jnp.float32
AXES = ("region", "sub")
VMEM = pltpu.VMEM
MIB = 1024 * 1024
I16 = jnp.int16
VMEM_LIMIT = 60 * MIB
STEP_LOCAL = 1024
STEP_MAIN = 1024
STEP_REST = 1536


def near_offset(neighbour):
    return neighbour + 1 if neighbour < 3 else 2 - neighbour


def shifted(value, steps):
    count = lax.axis_size(AXES)
    return lax.ppermute(value, AXES, [(s, (s + steps) % count) for s in range(count)])


def exchange_far(rows):
    return lax.all_to_all(rows, AXES, split_axis=0, concat_axis=0, tiled=True)


def dot(a, b):
    return lax.dot_general(a, b, (((1,), (0,)), ((), ())), preferred_element_type=F32)


def dot_nt(a, b):
    return lax.dot_general(a, b, (((1,), (1,)), ((), ())), preferred_element_type=F32)


def dot_tn(a, b):
    return lax.dot_general(a, b, (((0,), (0,)), ((), ())), preferred_element_type=F32)


def hot_rows(index_row, first, count):
    n = index_row.shape[1]
    block = jnp.broadcast_to(index_row - first, (16, n)).astype(I16)
    ids = lax.broadcasted_iota(jnp.int32, (16, n), 0).astype(I16)
    one, zero = jnp.ones((16, n), BF), jnp.zeros((16, n), BF)
    return jnp.concatenate(
        [jnp.where(block == ids + I16(16 * k), one, zero) for k in range(count // 16)], axis=0
    )


def hot_columns(index_lanes, first, count):
    lane = lax.broadcasted_iota(jnp.int32, index_lanes.shape, 1).astype(I16)
    one, zero = jnp.ones(index_lanes.shape, BF), jnp.zeros(index_lanes.shape, BF)
    parts = [
        jnp.where(index_lanes == lane + I16(128 * k + first), one, zero) for k in range(count // 128)
    ]
    return jnp.concatenate(parts, axis=1)


def spread_lanes(index, lanes_ref):
    flipped = jnp.transpose(index, (1, 0))
    for j in range(index.shape[0]):
        lanes_ref[pl.ds(j * 128, 128), :] = jnp.broadcast_to(flipped[:, j : j + 1], (128, 128)).astype(I16)


def index_row(ref, t, step):
    per = step // 128
    return jnp.concatenate([ref[pl.ds(t * per + i, 1), :] for i in range(per)], axis=1)


def row_mean(x):
    return jnp.sum(x, axis=1, keepdims=True) * (1.0 / x.shape[1])


def normalise(mixed):
    centre = mixed - row_mean(mixed)
    spread = lax.rsqrt(row_mean(centre * centre) + 1e-05)
    return centre * spread, spread


def norm_back(scaled, normal, spread):
    return spread * (scaled - row_mean(scaled) - normal * row_mean(scaled * normal))


def silu_parts(x):
    sigma = 0.5 * jnp.tanh(0.5 * x) + 0.5
    active = x * sigma
    return active, sigma + active * (1.0 - sigma)


def step_rows(t, step):
    return pl.ds(pl.multiple_of(t * step, step), step)


def piece(t, step, src, dst, sems):
    rows = step_rows(t, step)
    return pltpu.make_async_copy(src.at[rows], dst.at[rows], sems.at[t])


def live_rows(counts_ref, t, step):
    position = lax.broadcasted_iota(jnp.int32, (step, 1), 0)
    tiles = step // TILE
    limit = counts_ref[t * tiles]
    for i in range(1, tiles):
        limit = jnp.where(position >= i * TILE, counts_ref[t * tiles + i] + i * TILE, limit)
    return position < limit


def fetch(sems, *pairs):
    copies = [pltpu.make_async_copy(s, d, sems.at[i]) for i, (s, d) in enumerate(pairs)]
    for c in copies:
        c.start()
    return copies


def gather_kernel(nodes_hbm, list_hbm, *refs):
    outs, (nodes, slots, sems) = refs[:7], refs[7:]
    for c in fetch(sems, (list_hbm, slots), (nodes_hbm, nodes)):
        c.wait()
    hot = hot_rows(slots[...], 0, nodes.shape[0])
    rows = dot_tn(hot, nodes[...]).astype(BF)
    for i in range(6):
        outs[i][...] = rows[i * NEAR : (i + 1) * NEAR]
    outs[6][...] = rows[NEAR_TOTAL:]


def local_kernel(
    nodes_hbm, sender_hbm, receiver_hbm, w1_hbm, edges_hbm, part_hbm,
    nodes, sender, receiver, w1, edges, part, slanes, rlanes, table, sems, in_sem, out_sem,
):
    step = STEP_LOCAL
    steps = edges.shape[0] // step
    count, width = nodes.shape
    first = fetch(sems, (sender_hbm, sender), (receiver_hbm, receiver), (nodes_hbm, nodes), (w1_hbm, w1))
    for t in range(steps):
        piece(t, step, edges_hbm, edges, in_sem).start()
    for c in first[:2]:
        c.wait()
    spread_lanes(sender[...], slanes)
    spread_lanes(receiver[...], rlanes)
    for c in first[2:]:
        c.wait()
    table[:count, :] = dot(nodes[...], w1[width : 2 * width, :]).astype(BF)
    table[count:, :] = dot(nodes[...], w1[2 * width :, :]).astype(BF)

    def body(t, carry):
        rows = step_rows(t, step)
        piece(t, step, edges_hbm, edges, in_sem).wait()
        hot = jnp.concatenate(
            [hot_columns(slanes[rows, :], 0, count), hot_columns(rlanes[rows, :], 0, count)], axis=1
        )
        total = dot(hot, table[...]) + dot(edges[rows, :], w1[:width, :])
        part[rows, :] = total.astype(BF)
        piece(t, step, part, part_hbm, out_sem).start()
        return carry

    lax.fori_loop(0, steps, body, 0)
    for t in range(steps):
        piece(t, step, part, part_hbm, out_sem).wait()


def main_kernel(
    counts_ref, n0, n1, n2, n3, n4, n5, far_hbm, sender_hbm, receiver_hbm,
    w1_hbm, w2_hbm, gain_hbm, nw1_hbm, nw2_hbm, ngain_hbm, nodes_hbm, ncot_hbm,
    part_hbm, edges_hbm, cot_hbm,
    edge_out_hbm, node_out_hbm, hgrad_hbm, r0, r1, r2, r3, r4, r5, rfar, direct_hbm,
    arrived, sender, receiver, w1s, w2, gain_ref, nw1, nw2, ngain, nodes, ncot,
    part, edges, cot, eout, normals, slopes, hgrad, slanes, rlanes, spreads, table, sums, aggregate,
    agrad, node_out, direct, w2t,
    sems, node_sem, part_sem, edges_sem, cot_sem, eout_sem, hgrad_sem, last_sem,
):
    step = STEP_MAIN
    steps = edges.shape[0] // step
    count, width = nodes.shape
    halo = table.shape[0]
    fed = arrived.shape[0]
    near = [(n, arrived.at[pl.ds(i * NEAR, NEAR)]) for i, n in enumerate((n0, n1, n2, n3, n4, n5))]
    first = fetch(
        sems, (sender_hbm, sender), (receiver_hbm, receiver), (w1_hbm.at[pl.ds(width, width)], w1s), *near,
        (far_hbm, arrived.at[pl.ds(NEAR_TOTAL, fed - NEAR_TOTAL)]),
        (w2_hbm, w2), (gain_hbm, gain_ref),
    )
    for t in range(steps):
        piece(t, step, part_hbm, part, part_sem).start()
    for t in range(steps):
        piece(t, step, edges_hbm, edges, edges_sem).start()
    later = fetch(
        node_sem, (nw1_hbm, nw1), (nw2_hbm, nw2), (ngain_hbm, ngain), (nodes_hbm, nodes), (ncot_hbm, ncot),
    )
    for t in range(steps):
        piece(t, step, cot_hbm, cot, cot_sem).start()
    for c in first[:2]:
        c.wait()
    spread_lanes(sender[...], slanes)
    spread_lanes(receiver[...], rlanes)
    aggregate[...] = jnp.zeros_like(aggregate)
    sums[...] = jnp.zeros_like(sums)
    for c in first[2:]:
        c.wait()
    table[:fed, :] = dot(arrived[...], w1s[...]).astype(BF)
    table[fed:, :] = jnp.zeros((halo - fed, width), BF)
    gain = gain_ref[...]

    def forward(t, carry):
        rows = step_rows(t, step)
        piece(t, step, part_hbm, part, part_sem).wait()
        hot = hot_columns(slanes[rows, :], count, halo)
        hidden = part[rows, :].astype(F32) + dot(hot, table[...])
        active, slope = silu_parts(hidden)
        slopes[rows, :] = slope.astype(BF)
        normal, spread = normalise(dot(active.astype(BF), w2[...]))
        normals[rows, :] = normal.astype(BF)
        spreads[rows, :] = spread
        message = jnp.where(live_rows(counts_ref, t, step), normal * gain, 0.0)
        piece(t, step, edges_hbm, edges, edges_sem).wait()
        eout[rows, :] = (edges[rows, :].astype(F32) + message).astype(BF)
        into = hot_rows(index_row(receiver, t, step), 0, count)
        aggregate[...] += dot(into, message.astype(BF))
        piece(t, step, eout, edge_out_hbm, eout_sem).start()
        return carry

    lax.fori_loop(0, steps, forward, 0)
    for c in later:
        c.wait()

    node_hidden = dot(nodes[...], nw1[:width, :]) + dot(aggregate[...].astype(BF), nw1[width:, :])
    active, node_slope = silu_parts(node_hidden)
    node_mixed = dot(active.astype(BF), nw2[...])
    normal, spread = normalise(node_mixed)
    node_out[...] = (nodes[...].astype(F32) + normal * ngain[...]).astype(BF)
    node_cot = ncot[...].astype(F32)
    mixed_grad = norm_back(node_cot * ngain[...], normal, spread).astype(BF)
    hidden_grad = (dot_nt(mixed_grad, nw2[...]) * node_slope).astype(BF)
    direct[...] = node_cot + dot_nt(hidden_grad, nw1[:width, :])
    agrad[...] = dot_nt(hidden_grad, nw1[width:, :]).astype(BF)
    ends = fetch(last_sem, (node_out, node_out_hbm), (direct, direct_hbm))
    w2t[...] = jnp.transpose(w2[...], (1, 0))

    def backward(t, carry):
        rows = step_rows(t, step)
        upper = dot(hot_columns(rlanes[rows, :], 0, count), agrad[...])
        piece(t, step, cot_hbm, cot, cot_sem).wait()
        live = live_rows(counts_ref, t, step)
        scaled = jnp.where(live, (upper + cot[rows, :].astype(F32)) * gain, 0.0)
        grad = norm_back(scaled, normals[rows, :].astype(F32), spreads[rows, :]).astype(BF)
        hg = (dot(grad, w2t[...]) * slopes[rows, :].astype(F32)).astype(BF)
        hgrad[rows, :] = hg
        sums[...] += dot(hot_rows(index_row(sender, t, step), count, halo), hg)
        piece(t, step, hgrad, hgrad_hbm, hgrad_sem).start()
        return carry

    lax.fori_loop(0, steps, backward, 0)
    back = dot_nt(sums[...].astype(BF), w1s[...]).astype(BF)
    for i, ref in enumerate((r0, r1, r2, r3, r4, r5)):
        ref[...] = back[i * NEAR : (i + 1) * NEAR]
    rfar[...] = back[NEAR_TOTAL:fed]
    for t in range(steps):
        piece(t, step, eout, edge_out_hbm, eout_sem).wait()
        piece(t, step, hgrad, hgrad_hbm, hgrad_sem).wait()
    for c in ends:
        c.wait()


def rest_kernel(
    sender_hbm, receiver_hbm, w1_hbm, direct_hbm, hgrad_hbm, cot_hbm, grad_hbm, owned_hbm,
    sender, receiver, w1, direct, hgrad, cot, sums, w1t, sems, h_sem, c_sem, out_sem, last_sem,
):
    step = STEP_REST
    steps = hgrad.shape[0] // step
    count, width = direct.shape
    first = fetch(sems, (sender_hbm, sender), (receiver_hbm, receiver), (w1_hbm, w1), (direct_hbm, direct))
    for t in range(steps):
        piece(t, step, hgrad_hbm, hgrad, h_sem).start()
        piece(t, step, cot_hbm, cot, c_sem).start()
    sums[...] = jnp.zeros_like(sums)
    for c in first:
        c.wait()
    w1t[...] = jnp.transpose(w1[:width, :], (1, 0))

    def body(t, carry):
        rows = step_rows(t, step)
        piece(t, step, hgrad_hbm, hgrad, h_sem).wait()
        piece(t, step, cot_hbm, cot, c_sem).wait()
        hg = hgrad[rows, :]
        cot[rows, :] = (cot[rows, :].astype(F32) + dot(hg, w1t[...])).astype(BF)
        hot = jnp.concatenate(
            [hot_rows(index_row(sender, t, step), 0, count), hot_rows(index_row(receiver, t, step), 0, count)],
            axis=0,
        )
        sums[...] += dot(hot, hg)
        piece(t, step, cot, grad_hbm, out_sem).start()
        return carry

    lax.fori_loop(0, steps, body, 0)
    direct[...] = (
        direct[...]
        + dot_nt(sums[:count, :].astype(BF), w1[width : 2 * width, :])
        + dot_nt(sums[count:, :].astype(BF), w1[2 * width :, :])
    )
    for c in fetch(last_sem, (direct, owned_hbm)):
        c.wait()
    for t in range(steps):
        piece(t, step, cot, grad_hbm, out_sem).wait()


def final_kernel(
    list_hbm, owned_hbm, n0, n1, n2, n3, n4, n5, far_hbm, out_hbm,
    slots, owned, returned, out, sems, last_sem,
):
    fed = returned.shape[0]
    near = [(n, returned.at[pl.ds(i * NEAR, NEAR)]) for i, n in enumerate((n0, n1, n2, n3, n4, n5))]
    for c in fetch(
        sems, (list_hbm, slots), (owned_hbm, owned), *near,
        (far_hbm, returned.at[pl.ds(NEAR_TOTAL, fed - NEAR_TOTAL)]),
    ):
        c.wait()
    hot = hot_rows(slots[...], 0, owned.shape[0])
    out[...] = (owned[...] + dot(hot, returned[...])).astype(BF)
    for c in fetch(last_sem, (out, out_hbm)):
        c.wait()


def kernel_call(body, outs, in_specs, out_specs, scratch, flops, moved):
    return pl.pallas_call(
        body,
        out_shape=outs,
        in_specs=in_specs,
        out_specs=out_specs,
        scratch_shapes=scratch,
        compiler_params=pltpu.CompilerParams(vmem_limit_bytes=VMEM_LIMIT),
        cost_estimate=pl.CostEstimate(flops=flops, bytes_accessed=moved, transcendentals=0),
    )


def on_device(
    nodes, edges, sender, receiver, tile_counts, send_list, edge_w1, edge_w2, edge_gain,
    node_w1, node_w2, node_gain, node_cotangent, edge_cotangent,
):
    count, width = nodes.shape
    slots = edges.shape[0]
    halo = send_list.shape[1]
    far_rows = halo - NEAR_TOTAL
    padded = -(-halo // 256) * 256
    v = pl.BlockSpec(memory_space=pltpu.VMEM)
    s = pl.BlockSpec(memory_space=pltpu.SMEM)
    a = pl.BlockSpec(memory_space=pl.ANY)
    sds = jax.ShapeDtypeStruct
    sem = lambda n: pltpu.SemaphoreType.DMA((n,))
    near_shapes = [sds((NEAR, width), BF)] * 6 + [sds((far_rows, width), BF)]
    big = sds((slots, width), BF)
    wide = VMEM((slots, width), BF)
    lanes = VMEM((slots, 128), I16)
    index = VMEM((slots // 128, 128), jnp.int32)
    listed = VMEM((1, halo), jnp.int32)
    block = VMEM((count, width), BF)
    block32 = VMEM((count, width), F32)
    mat = VMEM((width, width), BF)
    vec = VMEM((1, width), F32)
    w1 = VMEM((3 * width, width), BF)
    square = 2 * count * width * width

    sender = sender.reshape(slots // 128, 128)
    receiver = receiver.reshape(slots // 128, 128)
    gain = edge_gain.reshape(1, width)
    ngain = node_gain.reshape(1, width)

    leaving = kernel_call(
        gather_kernel, near_shapes, [a, a], [v] * 7, [block, listed, sem(2)],
        2 * halo * count * width, 2 * MIB,
    )(nodes, send_list)
    arrived = [shifted(leaving[i], near_offset(i)) for i in range(6)]
    far = exchange_far(leaving[6])

    n = slots // STEP_LOCAL
    part = kernel_call(
        local_kernel, big, [a] * 5, a,
        [block, index, index, w1, wide, wide, lanes, lanes, VMEM((2 * count, width), BF), sem(4), sem(n), sem(n)],
        20 * square, 8 * MIB,
    )(nodes, sender, receiver, edge_w1, edges)

    n = slots // STEP_MAIN
    outs = kernel_call(
        main_kernel,
        [big, sds((count, width), BF), big] + near_shapes + [sds((count, width), F32)],
        [s] + [a] * 20,
        [a, a, a] + [v] * 7 + [a],
        [VMEM((halo, width), BF), index, index, mat, mat, vec, VMEM((2 * width, width), BF), mat, vec, block, block]
        + [wide] * 7
        + [lanes, lanes, VMEM((slots, 1), F32), VMEM((padded, width), BF), VMEM((padded, width), F32),
           block32, block, block, block32, mat]
        + [sem(12), sem(5)] + [sem(n)] * 5 + [sem(2)],
        50 * square, 20 * MIB,
    )(
        tile_counts, *arrived, far, sender, receiver, edge_w1, edge_w2, gain, node_w1, node_w2, ngain,
        nodes, node_cotangent, part, edges, edge_cotangent,
    )
    edge_out, node_out, hgrad = outs[:3]
    back = outs[3:10]
    direct = outs[10]
    returned = [shifted(back[i], -near_offset(i)) for i in range(6)]
    far_back = exchange_far(back[6])

    n = slots // STEP_REST
    grad_edges, owned = kernel_call(
        rest_kernel, [big, sds((count, width), F32)], [a] * 6, [a, a],
        [index, index, w1, block32, wide, wide, VMEM((2 * count, width), F32), mat, sem(4), sem(n), sem(n), sem(n), sem(1)],
        20 * square, 12 * MIB,
    )(sender, receiver, edge_w1, direct, hgrad, edge_cotangent)

    grad_nodes = kernel_call(
        final_kernel, sds((count, width), BF), [a] * 9, a,
        [listed, block32, VMEM((halo, width), BF), block, sem(9), sem(1)], 2 * square, 3 * MIB,
    )(send_list, owned, *returned, far_back)
    return edge_out, node_out, grad_edges, grad_nodes


def solution(mesh):
    rows = P(AXES, None)
    flat = P(AXES)
    in_specs = (
        rows, rows, flat, flat, flat, rows, P(), P(), P(), P(), P(), P(), rows, rows,
    )
    return jax.shard_map(
        on_device, mesh=mesh, in_specs=in_specs, out_specs=(rows,) * 4, check_vma=False
    )
```

```python
import functools

import jax
import jax.numpy as jnp
from jax import lax
from jax.experimental import pallas as pl
from jax.experimental.pallas import tpu as pltpu
from jax.sharding import PartitionSpec as P

NEAR = 80
NEAR_TOTAL = 480
TILE = 256
BF = jnp.bfloat16
F32 = jnp.float32
AXES = ("region", "sub")
VMEM = pltpu.VMEM
MIB = 1024 * 1024
RETURN_ORDER = (3, 4, 5, 0, 1, 2)
I16 = jnp.int16
VMEM_LIMIT = 60 * MIB
SUB = 256
STEP_LOCAL = 1024
STEP_MAIN = 1024
STEP_REST = 1536


def near_offset(neighbour):
    return neighbour + 1 if neighbour < 3 else 2 - neighbour


def shifted(value, steps):
    count = lax.axis_size(AXES)
    return lax.ppermute(value, AXES, [(s, (s + steps) % count) for s in range(count)])


def exchange_far(rows):
    return lax.all_to_all(rows, AXES, split_axis=0, concat_axis=0, tiled=True)


def dot(a, b):
    return lax.dot_general(a, b, (((1,), (0,)), ((), ())), preferred_element_type=F32)


def dot_nt(a, b):
    return lax.dot_general(a, b, (((1,), (1,)), ((), ())), preferred_element_type=F32)


def dot_tn(a, b):
    return lax.dot_general(a, b, (((0,), (0,)), ((), ())), preferred_element_type=F32)


def hot_rows(index_row, first, count):
    n = index_row.shape[1]
    block = jnp.broadcast_to(index_row - first, (16, n)).astype(I16)
    ids = lax.broadcasted_iota(jnp.int32, (16, n), 0).astype(I16)
    one, zero = jnp.ones((16, n), BF), jnp.zeros((16, n), BF)
    return jnp.concatenate(
        [jnp.where(block == ids + I16(16 * k), one, zero) for k in range(count // 16)], axis=0
    )


def hot_columns(index_lanes, first, count):
    lane = lax.broadcasted_iota(jnp.int32, index_lanes.shape, 1).astype(I16)
    one, zero = jnp.ones(index_lanes.shape, BF), jnp.zeros(index_lanes.shape, BF)
    parts = [
        jnp.where(index_lanes == lane + I16(128 * k + first), one, zero) for k in range(count // 128)
    ]
    return jnp.concatenate(parts, axis=1)


def spread_lanes(index, lanes_ref):
    flipped = jnp.transpose(index, (1, 0))
    for j in range(index.shape[0]):
        lanes_ref[pl.ds(j * 128, 128), :] = jnp.broadcast_to(flipped[:, j : j + 1], (128, 128)).astype(I16)


def index_row(ref, t, step):
    per = step // 128
    return jnp.concatenate([ref[pl.ds(t * per + i, 1), :] for i in range(per)], axis=1)


def row_mean(x):
    return jnp.sum(x, axis=1, keepdims=True) * (1.0 / x.shape[1])


def normalise(mixed):
    centre = mixed - row_mean(mixed)
    spread = lax.rsqrt(row_mean(centre * centre) + 1e-05)
    return centre * spread, spread


def norm_back(scaled, normal, spread):
    return spread * (scaled - row_mean(scaled) - normal * row_mean(scaled * normal))


def silu_parts(x):
    sigma = 0.5 * jnp.tanh(0.5 * x) + 0.5
    active = x * sigma
    return active, sigma + active * (1.0 - sigma)


def step_rows(t, step):
    return pl.ds(pl.multiple_of(t * step, step), step)


def piece(t, step, src, dst, sems):
    rows = step_rows(t, step)
    return pltpu.make_async_copy(src.at[rows], dst.at[rows], sems.at[t])


def live_rows(counts_ref, t, step):
    position = lax.broadcasted_iota(jnp.int32, (step, 1), 0)
    tiles = step // TILE
    limit = counts_ref[t * tiles]
    for i in range(1, tiles):
        limit = jnp.where(position >= i * TILE, counts_ref[t * tiles + i] + i * TILE, limit)
    return position < limit


def live_part(counts_ref, t, step, i):
    position = lax.broadcasted_iota(jnp.int32, (SUB, 1), 0)
    tile = t * (step // TILE) + i * SUB // TILE
    limit = counts_ref[tile]
    for k in range(1, SUB // TILE):
        limit = jnp.where(position >= k * TILE, counts_ref[tile + k] + k * TILE, limit)
    return position < limit


def fetch(sems, *pairs):
    copies = [pltpu.make_async_copy(s, d, sems.at[i]) for i, (s, d) in enumerate(pairs)]
    for c in copies:
        c.start()
    return copies


def pack_far(rows, wide_ref, out_ref):
    quarters = rows.shape[1] // 128
    for c in range(quarters):
        wide_ref[pl.ds(c, rows.shape[0], stride=quarters), :] = rows[:, c * 128 : (c + 1) * 128]
    out_ref[...] = wide_ref[...].reshape(out_ref.shape).astype(BF)


def unpack_far(packed_ref, wide_ref, out_ref):
    wide_ref[...] = packed_ref[...].astype(F32).reshape(wide_ref.shape)
    quarters = out_ref.shape[1] // 128
    count = wide_ref.shape[0] // quarters
    for c in range(quarters):
        out_ref[NEAR_TOTAL:, c * 128 : (c + 1) * 128] = wide_ref[
            pl.ds(c, count, stride=quarters), :
        ].astype(BF)


def gather_kernel(nodes_hbm, list_hbm, *refs):
    outs, (nodes, slots, wide, sems) = refs[:7], refs[7:]
    for c in fetch(sems, (list_hbm, slots), (nodes_hbm, nodes)):
        c.wait()
    hot = hot_rows(slots[...], 0, nodes.shape[0])
    rows = dot_tn(hot, nodes[...])
    for i in range(6):
        outs[i][...] = rows[i * NEAR : (i + 1) * NEAR].astype(BF)
    pack_far(rows[NEAR_TOTAL:], wide, outs[6])


def local_kernel(
    nodes_hbm, sender_hbm, receiver_hbm, w1_hbm, edges_hbm, part_hbm,
    nodes, sender, receiver, w1, edges, part, slanes, rlanes, table, sems, in_sem, out_sem,
):
    step = STEP_LOCAL
    steps = edges.shape[0] // step
    count, width = nodes.shape
    first = fetch(sems, (sender_hbm, sender), (receiver_hbm, receiver), (nodes_hbm, nodes), (w1_hbm, w1))
    for t in range(steps):
        piece(t, step, edges_hbm, edges, in_sem).start()
    for c in first[:2]:
        c.wait()
    spread_lanes(sender[...], slanes)
    spread_lanes(receiver[...], rlanes)
    for c in first[2:]:
        c.wait()
    table[:count, :] = dot(nodes[...], w1[width : 2 * width, :]).astype(BF)
    table[count:, :] = dot(nodes[...], w1[2 * width :, :]).astype(BF)

    def body(t, carry):
        rows = step_rows(t, step)
        piece(t, step, edges_hbm, edges, in_sem).wait()
        hot = jnp.concatenate(
            [hot_columns(slanes[rows, :], 0, count), hot_columns(rlanes[rows, :], 0, count)], axis=1
        )
        total = dot(hot, table[...]) + dot(edges[rows, :], w1[:width, :])
        part[rows, :] = total.astype(BF)
        piece(t, step, part, part_hbm, out_sem).start()
        return carry

    lax.fori_loop(0, steps, body, 0)
    for t in range(steps):
        piece(t, step, part, part_hbm, out_sem).wait()


def main_kernel(
    counts_hbm, n0, n1, n2, n3, n4, n5, far_hbm, sender_hbm, receiver_hbm,
    w1_hbm, w2_hbm, gain_hbm, nw1_hbm, nw2_hbm, ngain_hbm, nodes_hbm, ncot_hbm,
    part_hbm, edges_hbm, cot_hbm,
    edge_out_hbm, node_out_hbm, hgrad_hbm, r0, r1, r2, r3, r4, r5, rfar, direct_hbm,
    counts_ref, far_packed, far_wide, arrived, sender, receiver, w1s, w2, gain_ref, nw1, nw2, ngain, nodes, ncot,
    part, edges, cot, eout, normals, slopes, hgrad, slanes, rlanes, spreads, table, sums, aggregate,
    agrad, node_out, direct, w2t, w2c, messages,
    sems, node_sem, part_sem, edges_sem, cot_sem, eout_sem, hgrad_sem, last_sem,
):
    step = STEP_MAIN
    steps = edges.shape[0] // step
    count, width = nodes.shape
    halo = table.shape[0]
    fed = arrived.shape[0]
    near = [(n, arrived.at[pl.ds(i * NEAR, NEAR)]) for i, n in enumerate((n0, n1, n2, n3, n4, n5))]
    first = fetch(
        sems, (sender_hbm, sender), (receiver_hbm, receiver), (w1_hbm.at[pl.ds(width, width)], w1s), *near,
        (far_hbm, far_packed), (counts_hbm, counts_ref), (w2_hbm, w2), (gain_hbm, gain_ref),
    )
    for t in range(steps):
        piece(t, step, part_hbm, part, part_sem).start()
    for t in range(steps):
        piece(t, step, edges_hbm, edges, edges_sem).start()
    later = fetch(
        node_sem, (nw1_hbm, nw1), (nw2_hbm, nw2), (ngain_hbm, ngain), (nodes_hbm, nodes), (ncot_hbm, ncot),
    )
    for t in range(steps):
        piece(t, step, cot_hbm, cot, cot_sem).start()
    for c in first[:2]:
        c.wait()
    spread_lanes(sender[...], slanes)
    spread_lanes(receiver[...], rlanes)
    aggregate[...] = jnp.zeros_like(aggregate)
    sums[...] = jnp.zeros_like(sums)
    for c in first[2:]:
        c.wait()
    unpack_far(far_packed, far_wide, arrived)
    table[:fed, :] = dot(arrived[...], w1s[...]).astype(BF)
    table[fed:, :] = jnp.zeros((halo - fed, width), BF)
    gain = gain_ref[...]

    w2c[...] = (w2[...].astype(F32) - row_mean(w2[...].astype(F32))).astype(BF)
    messages[...] = jnp.zeros_like(messages)
    subs = step // SUB

    def part_of(t, i):
        return pl.ds(pl.multiple_of(t * step + i * SUB, SUB), SUB)

    def collect(t):
        into = hot_rows(index_row(receiver, t, step), 0, count)
        aggregate[...] += dot(into, messages[...])

    def forward(t, carry):
        piece(t, step, part_hbm, part, part_sem).wait()
        piece(t, step, edges_hbm, edges, edges_sem).wait()
        collect(jnp.maximum(t - 1, 0))
        hidden, centre = {}, {}
        for i in range(subs + 2):
            if i < subs:
                rows = part_of(t, i)
                hot = hot_columns(slanes[rows, :], count, halo)
                hidden[i] = part[rows, :].astype(F32) + dot(hot, table[...])
            if 0 <= i - 1 < subs:
                active, slope = silu_parts(hidden.pop(i - 1))
                slopes[part_of(t, i - 1), :] = slope.astype(BF)
                centre[i - 1] = dot(active.astype(BF), w2c[...])
            if i >= 2:
                rows = part_of(t, i - 2)
                c = centre.pop(i - 2)
                spread = lax.rsqrt(row_mean(c * c) + 1e-05)
                normal = c * spread
                normals[rows, :] = normal.astype(BF)
                spreads[rows, :] = spread
                message = jnp.where(live_part(counts_ref, t, step, i - 2), normal * gain, 0.0)
                eout[rows, :] = (edges[rows, :].astype(F32) + message).astype(BF)
                messages[(i - 2) * SUB : (i - 1) * SUB, :] = message.astype(BF)
        piece(t, step, eout, edge_out_hbm, eout_sem).start()
        return carry

    lax.fori_loop(0, steps, forward, 0)
    collect(steps - 1)
    for c in later:
        c.wait()

    node_hidden = dot(nodes[...], nw1[:width, :]) + dot(aggregate[...].astype(BF), nw1[width:, :])
    active, node_slope = silu_parts(node_hidden)
    node_mixed = dot(active.astype(BF), nw2[...])
    normal, spread = normalise(node_mixed)
    node_out[...] = (nodes[...].astype(F32) + normal * ngain[...]).astype(BF)
    node_cot = ncot[...].astype(F32)
    mixed_grad = norm_back(node_cot * ngain[...], normal, spread).astype(BF)
    hidden_grad = (dot_nt(mixed_grad, nw2[...]) * node_slope).astype(BF)
    direct[...] = node_cot + dot_nt(hidden_grad, nw1[:width, :])
    agrad[...] = dot_nt(hidden_grad, nw1[width:, :]).astype(BF)
    ends = fetch(last_sem, (node_out, node_out_hbm), (direct, direct_hbm))
    w2t[...] = jnp.transpose(w2[...], (1, 0))

    hgrad[step_rows(0, step), :] = jnp.zeros((step, width), BF)

    def gather_back(t):
        hg = hgrad[step_rows(t, step), :]
        sums[...] += dot(hot_rows(index_row(sender, t, step), count, halo), hg)

    def backward(t, carry):
        piece(t, step, cot_hbm, cot, cot_sem).wait()
        gather_back(jnp.maximum(t - 1, 0))
        upper, grad = {}, {}
        for i in range(subs + 2):
            if i < subs:
                upper[i] = dot(hot_columns(rlanes[part_of(t, i), :], 0, count), agrad[...])
            if 0 <= i - 1 < subs:
                rows = part_of(t, i - 1)
                live = live_part(counts_ref, t, step, i - 1)
                scaled = jnp.where(live, (upper.pop(i - 1) + cot[rows, :].astype(F32)) * gain, 0.0)
                grad[i - 1] = norm_back(scaled, normals[rows, :].astype(F32), spreads[rows, :]).astype(BF)
            if i >= 2:
                rows = part_of(t, i - 2)
                hgrad[rows, :] = (dot(grad.pop(i - 2), w2t[...]) * slopes[rows, :].astype(F32)).astype(BF)
        piece(t, step, hgrad, hgrad_hbm, hgrad_sem).start()
        return carry

    lax.fori_loop(0, steps, backward, 0)
    gather_back(steps - 1)
    back = dot_nt(sums[...].astype(BF), w1s[...])
    for i, ref in zip(RETURN_ORDER, (r0, r1, r2, r3, r4, r5)):
        ref[...] = back[i * NEAR : (i + 1) * NEAR].astype(BF)
    pack_far(back[NEAR_TOTAL:fed], far_wide, rfar)
    for t in range(steps):
        piece(t, step, eout, edge_out_hbm, eout_sem).wait()
        piece(t, step, hgrad, hgrad_hbm, hgrad_sem).wait()
    for c in ends:
        c.wait()


def rest_kernel(
    sender_hbm, receiver_hbm, w1_hbm, direct_hbm, hgrad_hbm, cot_hbm, grad_hbm, owned_hbm,
    sender, receiver, w1, direct, hgrad, cot, sums, w1t, sems, late_sem, h_sem, c_sem, out_sem, last_sem,
):
    step = STEP_REST
    steps = hgrad.shape[0] // step
    count, width = direct.shape
    top, bottom = pl.ds(0, width), pl.ds(width, 2 * width)
    first = fetch(sems, (sender_hbm, sender), (receiver_hbm, receiver), (w1_hbm.at[top], w1.at[top]))
    for t in range(steps):
        piece(t, step, hgrad_hbm, hgrad, h_sem).start()
        piece(t, step, cot_hbm, cot, c_sem).start()
    later = fetch(late_sem, (w1_hbm.at[bottom], w1.at[bottom]), (direct_hbm, direct))
    sums[...] = jnp.zeros_like(sums)
    for c in first:
        c.wait()
    w1t[...] = jnp.transpose(w1[:width, :], (1, 0))

    def body(t, carry):
        rows = step_rows(t, step)
        piece(t, step, hgrad_hbm, hgrad, h_sem).wait()
        piece(t, step, cot_hbm, cot, c_sem).wait()
        hg = hgrad[rows, :]
        cot[rows, :] = (cot[rows, :].astype(F32) + dot(hg, w1t[...])).astype(BF)
        hot = jnp.concatenate(
            [hot_rows(index_row(sender, t, step), 0, count), hot_rows(index_row(receiver, t, step), 0, count)],
            axis=0,
        )
        sums[...] += dot(hot, hg)
        piece(t, step, cot, grad_hbm, out_sem).start()
        return carry

    lax.fori_loop(0, steps, body, 0)
    for c in later:
        c.wait()
    direct[...] = (
        direct[...]
        + dot_nt(sums[:count, :].astype(BF), w1[width : 2 * width, :])
        + dot_nt(sums[count:, :].astype(BF), w1[2 * width :, :])
    )
    for c in fetch(last_sem, (direct, owned_hbm)):
        c.wait()
    for t in range(steps):
        piece(t, step, cot, grad_hbm, out_sem).wait()


def final_kernel(
    list_hbm, owned_hbm, n0, n1, n2, n3, n4, n5, far_hbm, out_hbm,
    slots, owned, returned, out, far_packed, far_wide, sems, last_sem,
):
    near = [(n, returned.at[pl.ds(i * NEAR, NEAR)]) for i, n in enumerate((n0, n1, n2, n3, n4, n5))]
    first = fetch(sems, (list_hbm, slots), *near, (far_hbm, far_packed), (owned_hbm, owned))
    first[0].wait()
    hot = hot_rows(slots[...], 0, owned.shape[0])
    for c in first[1:]:
        c.wait()
    unpack_far(far_packed, far_wide, returned)
    out[...] = (owned[...] + dot(hot, returned[...])).astype(BF)
    for c in fetch(last_sem, (out, out_hbm)):
        c.wait()


def kernel_call(body, outs, in_specs, out_specs, scratch, flops, moved):
    return pl.pallas_call(
        body,
        out_shape=outs,
        in_specs=in_specs,
        out_specs=out_specs,
        scratch_shapes=scratch,
        compiler_params=pltpu.CompilerParams(vmem_limit_bytes=VMEM_LIMIT),
        cost_estimate=pl.CostEstimate(flops=flops, bytes_accessed=moved, transcendentals=0),
    )


def on_device(
    nodes, edges, sender, receiver, tile_counts, send_list, edge_w1, edge_w2, edge_gain,
    node_w1, node_w2, node_gain, node_cotangent, edge_cotangent,
):
    count, width = nodes.shape
    slots = edges.shape[0]
    halo = send_list.shape[1]
    far_rows = halo - NEAR_TOTAL
    far_shape = (lax.axis_size(AXES), far_rows * width // 128 // lax.axis_size(AXES), 128)
    padded = -(-halo // 256) * 256
    v = pl.BlockSpec(memory_space=pltpu.VMEM)
    a = pl.BlockSpec(memory_space=pl.ANY)
    sds = jax.ShapeDtypeStruct
    sem = lambda n: pltpu.SemaphoreType.DMA((n,))
    near_shapes = [sds((NEAR, width), BF)] * 6 + [sds(far_shape, BF)]
    big = sds((slots, width), BF)
    far_packed = VMEM(far_shape, BF)
    far_wide = VMEM((far_rows * width // 128, 128), F32)
    wide = VMEM((slots, width), BF)
    lanes = VMEM((slots, 128), I16)
    index = VMEM((slots // 128, 128), jnp.int32)
    listed = VMEM((1, halo), jnp.int32)
    block = VMEM((count, width), BF)
    block32 = VMEM((count, width), F32)
    mat = VMEM((width, width), BF)
    vec = VMEM((1, width), F32)
    w1 = VMEM((3 * width, width), BF)
    square = 2 * count * width * width

    sender = sender.reshape(slots // 128, 128)
    receiver = receiver.reshape(slots // 128, 128)
    gain = edge_gain.reshape(1, width)
    ngain = node_gain.reshape(1, width)

    leaving = kernel_call(
        gather_kernel, near_shapes, [a, a], [v] * 7, [block, listed, far_wide, sem(2)],
        2 * halo * count * width, 2 * MIB,
    )(nodes, send_list)
    arrived = [shifted(leaving[i], near_offset(i)) for i in range(6)]
    far = exchange_far(leaving[6])

    n = slots // STEP_LOCAL
    part = kernel_call(
        local_kernel, big, [a] * 5, a,
        [block, index, index, w1, wide, wide, lanes, lanes, VMEM((2 * count, width), BF), sem(4), sem(n), sem(n)],
        square, MIB,
    )(nodes, sender, receiver, edge_w1, edges)

    n = slots // STEP_MAIN
    outs = kernel_call(
        main_kernel,
        [big, sds((count, width), BF), big] + near_shapes + [sds((count, width), F32)],
        [a] * 21,
        [a, a, a] + [v] * 7 + [a],
        [pltpu.SMEM(tile_counts.shape, jnp.int32), far_packed, far_wide,
         VMEM((halo, width), BF), index, index, mat, mat, vec, VMEM((2 * width, width), BF), mat, vec, block, block]
        + [wide] * 7
        + [lanes, lanes, VMEM((slots, 1), F32), VMEM((padded, width), BF), VMEM((padded, width), F32),
           block32, block, block, block32, mat, mat, VMEM((STEP_MAIN, width), BF)]
        + [sem(13), sem(5)] + [sem(n)] * 5 + [sem(2)],
        50 * square, 20 * MIB,
    )(
        tile_counts, *arrived, far, sender, receiver, edge_w1, edge_w2, gain, node_w1, node_w2, ngain,
        nodes, node_cotangent, part, edges, edge_cotangent,
    )
    edge_out, node_out, hgrad = outs[:3]
    back = outs[3:10]
    direct = outs[10]
    made = {i: shifted(back[k], -near_offset(i)) for k, i in enumerate(RETURN_ORDER)}
    returned = [made[i] for i in range(6)]
    far_back = exchange_far(back[6])

    n = slots // STEP_REST
    grad_edges, owned = kernel_call(
        rest_kernel, [big, sds((count, width), F32)], [a] * 6, [a, a],
        [index, index, w1, block32, wide, wide, VMEM((2 * count, width), F32), mat, sem(3), sem(2), sem(n), sem(n), sem(n), sem(1)],
        square, MIB,
    )(sender, receiver, edge_w1, direct, hgrad, edge_cotangent)

    grad_nodes = kernel_call(
        final_kernel, sds((count, width), BF), [a] * 9, a,
        [listed, block32, VMEM((halo, width), BF), block, far_packed, far_wide, sem(9), sem(1)], 2 * square, 3 * MIB,
    )(send_list, owned, *returned, far_back)
    return edge_out, node_out, grad_edges, grad_nodes


def solution(mesh):
    rows = P(AXES, None)
    flat = P(AXES)
    in_specs = (
        rows, rows, flat, flat, flat, rows, P(), P(), P(), P(), P(), P(), rows, rows,
    )
    return jax.shard_map(
        on_device, mesh=mesh, in_specs=in_specs, out_specs=(rows,) * 4, check_vma=False
    )
```

```python
import functools

import jax
import jax.numpy as jnp
from jax import lax
from jax.experimental import pallas as pl
from jax.experimental.pallas import tpu as pltpu
from jax.sharding import PartitionSpec as P

NEAR = 80
NEAR_TOTAL = 480
TILE = 256
BF = jnp.bfloat16
F32 = jnp.float32
AXES = ("region", "sub")
VMEM = pltpu.VMEM
MIB = 1024 * 1024
RETURN_ORDER = (3, 4, 5, 0, 1, 2)
I16 = jnp.int16
VMEM_LIMIT = 60 * MIB
SUB = 256
STEP_LOCAL = 1024
STEP_MAIN = 1024
STEP_REST = 1024
WINDOW = 256


def near_offset(neighbour):
    return neighbour + 1 if neighbour < 3 else 2 - neighbour


def shifted(value, steps):
    count = lax.axis_size(AXES)
    return lax.ppermute(value, AXES, [(s, (s + steps) % count) for s in range(count)])


def exchange_far(rows):
    return lax.all_to_all(rows, AXES, split_axis=0, concat_axis=0, tiled=True)


def dot(a, b):
    return lax.dot_general(a, b, (((1,), (0,)), ((), ())), preferred_element_type=F32)


def dot_nt(a, b):
    return lax.dot_general(a, b, (((1,), (1,)), ((), ())), preferred_element_type=F32)


def dot_tn(a, b):
    return lax.dot_general(a, b, (((0,), (0,)), ((), ())), preferred_element_type=F32)


def hot_rows(index_row, first, count):
    n = index_row.shape[1]
    block = jnp.broadcast_to(index_row - first, (16, n)).astype(I16)
    ids = lax.broadcasted_iota(jnp.int32, (16, n), 0).astype(I16)
    one, zero = jnp.ones((16, n), BF), jnp.zeros((16, n), BF)
    return jnp.concatenate(
        [jnp.where(block == ids + I16(16 * k), one, zero) for k in range(count // 16)], axis=0
    )


def hot_columns(index_lanes, first, count):
    lane = lax.broadcasted_iota(jnp.int32, index_lanes.shape, 1).astype(I16)
    one, zero = jnp.ones(index_lanes.shape, BF), jnp.zeros(index_lanes.shape, BF)
    parts = [
        jnp.where(index_lanes == lane + I16(128 * k + first), one, zero) for k in range(count // 128)
    ]
    return jnp.concatenate(parts, axis=1)


def spread_lanes(index, lanes_ref):
    flipped = jnp.transpose(index, (1, 0))
    for j in range(index.shape[0]):
        lanes_ref[pl.ds(j * 128, 128), :] = jnp.broadcast_to(flipped[:, j : j + 1], (128, 128)).astype(I16)


def index_row(ref, t, step):
    per = step // 128
    return jnp.concatenate([ref[pl.ds(t * per + i, 1), :] for i in range(per)], axis=1)


def row_mean(x):
    return jnp.sum(x, axis=1, keepdims=True) * (1.0 / x.shape[1])


def normalise(mixed):
    centre = mixed - row_mean(mixed)
    spread = lax.rsqrt(row_mean(centre * centre) + 1e-05)
    return centre * spread, spread


def norm_back(scaled, normal, spread):
    return spread * (scaled - row_mean(scaled) - normal * row_mean(scaled * normal))


def silu_parts(x):
    sigma = 0.5 * jnp.tanh(0.5 * x) + 0.5
    active = x * sigma
    return active, sigma + active * (1.0 - sigma)


def receiver_window(ids_ref, t, step, count):
    per = step // 128
    first, last = ids_ref[t * per, 0], ids_ref[t * per + per - 1, 127]
    base = jnp.minimum(lax.shift_left(lax.shift_right_logical(first, 4), 4), count - WINDOW)
    return base, last - base < WINDOW


def step_rows(t, step):
    return pl.ds(pl.multiple_of(t * step, step), step)


def piece(t, step, src, dst, sems):
    rows = step_rows(t, step)
    return pltpu.make_async_copy(src.at[rows], dst.at[rows], sems.at[t])


def live_rows(counts_ref, t, step):
    position = lax.broadcasted_iota(jnp.int32, (step, 1), 0)
    tiles = step // TILE
    limit = counts_ref[t * tiles]
    for i in range(1, tiles):
        limit = jnp.where(position >= i * TILE, counts_ref[t * tiles + i] + i * TILE, limit)
    return position < limit


def live_part(counts_ref, t, step, i):
    position = lax.broadcasted_iota(jnp.int32, (SUB, 1), 0)
    tile = t * (step // TILE) + i * SUB // TILE
    limit = counts_ref[tile]
    for k in range(1, SUB // TILE):
        limit = jnp.where(position >= k * TILE, counts_ref[tile + k] + k * TILE, limit)
    return position < limit


def fetch(sems, *pairs):
    copies = [pltpu.make_async_copy(s, d, sems.at[i]) for i, (s, d) in enumerate(pairs)]
    for c in copies:
        c.start()
    return copies


def pack_far(rows, wide_ref, out_ref):
    quarters = rows.shape[1] // 128
    for c in range(quarters):
        wide_ref[pl.ds(c, rows.shape[0], stride=quarters), :] = rows[:, c * 128 : (c + 1) * 128]
    out_ref[...] = wide_ref[...].reshape(out_ref.shape).astype(BF)


def unpack_far(packed_ref, wide_ref, out_ref):
    wide_ref[...] = packed_ref[...].astype(F32).reshape(wide_ref.shape)
    quarters = out_ref.shape[1] // 128
    count = wide_ref.shape[0] // quarters
    for c in range(quarters):
        out_ref[NEAR_TOTAL:, c * 128 : (c + 1) * 128] = wide_ref[
            pl.ds(c, count, stride=quarters), :
        ].astype(BF)


def gather_kernel(nodes_hbm, list_hbm, *refs):
    outs, (nodes, slots, wide, sems) = refs[:7], refs[7:]
    for c in fetch(sems, (list_hbm, slots), (nodes_hbm, nodes)):
        c.wait()
    hot = hot_rows(slots[...], 0, nodes.shape[0])
    rows = dot_tn(hot, nodes[...])
    for i in range(6):
        outs[i][...] = rows[i * NEAR : (i + 1) * NEAR].astype(BF)
    pack_far(rows[NEAR_TOTAL:], wide, outs[6])


def local_kernel(
    nodes_hbm, sender_hbm, receiver_hbm, w1_hbm, edges_hbm, part_hbm,
    nodes, sender, receiver, w1, edges, part, slanes, rlanes, table, window, ids, sems, in_sem, out_sem,
):
    step = STEP_LOCAL
    steps = edges.shape[0] // step
    count, width = nodes.shape
    first = fetch(sems, (sender_hbm, sender), (receiver_hbm, receiver), (nodes_hbm, nodes), (w1_hbm, w1), (receiver_hbm, ids))
    for t in range(steps):
        piece(t, step, edges_hbm, edges, in_sem).start()
    for c in first[:2]:
        c.wait()
    spread_lanes(sender[...], slanes)
    spread_lanes(receiver[...], rlanes)
    for c in first[2:]:
        c.wait()
    table[:count, :] = dot(nodes[...], w1[width : 2 * width, :]).astype(BF)
    table[count:, :] = dot(nodes[...], w1[2 * width :, :]).astype(BF)

    def body(t, carry):
        rows = step_rows(t, step)
        piece(t, step, edges_hbm, edges, in_sem).wait()
        base, fits = receiver_window(ids, t, step, count)

        @pl.when(fits)
        def _():
            window[:count, :] = table[:count, :]
            window[count : count + WINDOW, :] = table[pl.ds(pl.multiple_of(count + base, 16), WINDOW), :]
            window[count + WINDOW :, :] = w1[:width, :]
            near = rlanes[rows, :] - base.astype(I16)
            joined = jnp.concatenate(
                [hot_columns(slanes[rows, :], 0, count), hot_columns(near, 0, WINDOW), edges[rows, :]], axis=1
            )
            part[rows, :] = dot(joined, window[...]).astype(BF)

        @pl.when(jnp.logical_not(fits))
        def _():
            hot = jnp.concatenate(
                [hot_columns(slanes[rows, :], 0, count), hot_columns(rlanes[rows, :], 0, count)], axis=1
            )
            part[rows, :] = (dot(hot, table[...]) + dot(edges[rows, :], w1[:width, :])).astype(BF)

        piece(t, step, part, part_hbm, out_sem).start()
        return carry

    lax.fori_loop(0, steps, body, 0)
    for t in range(steps):
        piece(t, step, part, part_hbm, out_sem).wait()


def main_kernel(
    counts_hbm, n0, n1, n2, n3, n4, n5, far_hbm, sender_hbm, receiver_hbm,
    w1_hbm, w2_hbm, gain_hbm, nw1_hbm, nw2_hbm, ngain_hbm, nodes_hbm, ncot_hbm,
    part_hbm, edges_hbm, cot_hbm,
    edge_out_hbm, node_out_hbm, hgrad_hbm, r0, r1, r2, r3, r4, r5, rfar, direct_hbm,
    counts_ref, far_packed, far_wide, arrived, sender, receiver, w1s, w2, gain_ref, nw1, nw2, ngain, nodes, ncot,
    part, edges, cot, eout, normals, slopes, hgrad, slanes, rlanes, spreads, table, sums, aggregate,
    agrad, node_out, direct, w2t, w2c, messages,
    sems, node_sem, part_sem, edges_sem, cot_sem, eout_sem, hgrad_sem, last_sem,
):
    step = STEP_MAIN
    steps = edges.shape[0] // step
    count, width = nodes.shape
    halo = table.shape[0]
    fed = arrived.shape[0]
    near = [(n, arrived.at[pl.ds(i * NEAR, NEAR)]) for i, n in enumerate((n0, n1, n2, n3, n4, n5))]
    first = fetch(
        sems, (sender_hbm, sender), (receiver_hbm, receiver), (w1_hbm.at[pl.ds(width, width)], w1s), *near,
        (far_hbm, far_packed), (counts_hbm, counts_ref), (w2_hbm, w2), (gain_hbm, gain_ref),
    )
    for t in range(steps):
        piece(t, step, part_hbm, part, part_sem).start()
    for t in range(steps):
        piece(t, step, edges_hbm, edges, edges_sem).start()
    later = fetch(
        node_sem, (nw1_hbm, nw1), (nw2_hbm, nw2), (ngain_hbm, ngain), (nodes_hbm, nodes), (ncot_hbm, ncot),
    )
    for t in range(steps):
        piece(t, step, cot_hbm, cot, cot_sem).start()
    for c in first[:2]:
        c.wait()
    spread_lanes(sender[...], slanes)
    spread_lanes(receiver[...], rlanes)
    aggregate[...] = jnp.zeros_like(aggregate)
    sums[...] = jnp.zeros_like(sums)
    for c in first[2:]:
        c.wait()
    unpack_far(far_packed, far_wide, arrived)
    table[:fed, :] = dot(arrived[...], w1s[...]).astype(BF)
    table[fed:, :] = jnp.zeros((halo - fed, width), BF)
    gain = gain_ref[...]

    w2c[...] = (w2[...].astype(F32) - row_mean(w2[...].astype(F32))).astype(BF)
    messages[...] = jnp.zeros_like(messages)
    subs = step // SUB

    def part_of(t, i):
        return pl.ds(pl.multiple_of(t * step + i * SUB, SUB), SUB)

    def collect(t):
        into = hot_rows(index_row(receiver, t, step), 0, count)
        aggregate[...] += dot(into, messages[...])

    def forward(t, carry):
        piece(t, step, part_hbm, part, part_sem).wait()
        piece(t, step, edges_hbm, edges, edges_sem).wait()
        collect(jnp.maximum(t - 1, 0))
        hidden, centre = {}, {}
        for i in range(subs + 2):
            if i < subs:
                rows = part_of(t, i)
                hot = hot_columns(slanes[rows, :], count, halo)
                hidden[i] = part[rows, :].astype(F32) + dot(hot, table[...])
            if 0 <= i - 1 < subs:
                active, slope = silu_parts(hidden.pop(i - 1))
                slopes[part_of(t, i - 1), :] = slope.astype(BF)
                centre[i - 1] = dot(active.astype(BF), w2c[...])
            if i >= 2:
                rows = part_of(t, i - 2)
                c = centre.pop(i - 2)
                spread = lax.rsqrt(row_mean(c * c) + 1e-05)
                normal = c * spread
                normals[rows, :] = normal.astype(BF)
                spreads[rows, :] = spread
                message = jnp.where(live_part(counts_ref, t, step, i - 2), normal * gain, 0.0)
                eout[rows, :] = (edges[rows, :].astype(F32) + message).astype(BF)
                messages[(i - 2) * SUB : (i - 1) * SUB, :] = message.astype(BF)
        piece(t, step, eout, edge_out_hbm, eout_sem).start()
        return carry

    lax.fori_loop(0, steps, forward, 0)
    collect(steps - 1)
    for c in later:
        c.wait()

    node_hidden = dot(nodes[...], nw1[:width, :]) + dot(aggregate[...].astype(BF), nw1[width:, :])
    active, node_slope = silu_parts(node_hidden)
    node_mixed = dot(active.astype(BF), nw2[...])
    normal, spread = normalise(node_mixed)
    node_out[...] = (nodes[...].astype(F32) + normal * ngain[...]).astype(BF)
    node_cot = ncot[...].astype(F32)
    mixed_grad = norm_back(node_cot * ngain[...], normal, spread).astype(BF)
    hidden_grad = (dot_nt(mixed_grad, nw2[...]) * node_slope).astype(BF)
    direct[...] = node_cot + dot_nt(hidden_grad, nw1[:width, :])
    agrad[...] = dot_nt(hidden_grad, nw1[width:, :]).astype(BF)
    ends = fetch(last_sem, (node_out, node_out_hbm), (direct, direct_hbm))
    w2t[...] = jnp.transpose(w2[...], (1, 0))

    hgrad[step_rows(0, step), :] = jnp.zeros((step, width), BF)

    def gather_back(t):
        hg = hgrad[step_rows(t, step), :]
        sums[...] += dot(hot_rows(index_row(sender, t, step), count, halo), hg)

    def backward(t, carry):
        piece(t, step, cot_hbm, cot, cot_sem).wait()
        gather_back(jnp.maximum(t - 1, 0))
        upper, grad = {}, {}
        for i in range(subs + 2):
            if i < subs:
                upper[i] = dot(hot_columns(rlanes[part_of(t, i), :], 0, count), agrad[...])
            if 0 <= i - 1 < subs:
                rows = part_of(t, i - 1)
                live = live_part(counts_ref, t, step, i - 1)
                scaled = jnp.where(live, (upper.pop(i - 1) + cot[rows, :].astype(F32)) * gain, 0.0)
                grad[i - 1] = norm_back(scaled, normals[rows, :].astype(F32), spreads[rows, :]).astype(BF)
            if i >= 2:
                rows = part_of(t, i - 2)
                hgrad[rows, :] = (dot(grad.pop(i - 2), w2t[...]) * slopes[rows, :].astype(F32)).astype(BF)
        piece(t, step, hgrad, hgrad_hbm, hgrad_sem).start()
        return carry

    lax.fori_loop(0, steps, backward, 0)
    gather_back(steps - 1)
    back = dot_nt(sums[...].astype(BF), w1s[...])
    for i, ref in zip(RETURN_ORDER, (r0, r1, r2, r3, r4, r5)):
        ref[...] = back[i * NEAR : (i + 1) * NEAR].astype(BF)
    pack_far(back[NEAR_TOTAL:fed], far_wide, rfar)
    for t in range(steps):
        piece(t, step, eout, edge_out_hbm, eout_sem).wait()
        piece(t, step, hgrad, hgrad_hbm, hgrad_sem).wait()
    for c in ends:
        c.wait()


def rest_kernel(
    sender_hbm, receiver_hbm, w1_hbm, direct_hbm, hgrad_hbm, cot_hbm, grad_hbm, owned_hbm,
    sender, receiver, w1, direct, hgrad, cot, sums, w1t, ids, sems, late_sem, h_sem, c_sem, out_sem, last_sem,
):
    step = STEP_REST
    steps = hgrad.shape[0] // step
    count, width = direct.shape
    top, bottom = pl.ds(0, width), pl.ds(width, 2 * width)
    first = fetch(sems, (sender_hbm, sender), (receiver_hbm, receiver), (w1_hbm.at[top], w1.at[top]), (receiver_hbm, ids))
    for t in range(steps):
        piece(t, step, hgrad_hbm, hgrad, h_sem).start()
        piece(t, step, cot_hbm, cot, c_sem).start()
    later = fetch(late_sem, (w1_hbm.at[bottom], w1.at[bottom]), (direct_hbm, direct))
    sums[...] = jnp.zeros_like(sums)
    for c in first:
        c.wait()
    w1t[...] = jnp.transpose(w1[:width, :], (1, 0))

    def body(t, carry):
        rows = step_rows(t, step)
        piece(t, step, hgrad_hbm, hgrad, h_sem).wait()
        piece(t, step, cot_hbm, cot, c_sem).wait()
        hg = hgrad[rows, :]
        cot[rows, :] = (cot[rows, :].astype(F32) + dot(hg, w1t[...])).astype(BF)
        base, fits = receiver_window(ids, t, step, count)

        @pl.when(fits)
        def _():
            hot = jnp.concatenate(
                [hot_rows(index_row(sender, t, step), 0, count), hot_rows(index_row(receiver, t, step), base, WINDOW)],
                axis=0,
            )
            total = dot(hot, hg)
            sums[:count, :] += total[:count]
            sums[pl.ds(pl.multiple_of(count + base, 16), WINDOW), :] += total[count:]

        @pl.when(jnp.logical_not(fits))
        def _():
            hot = jnp.concatenate(
                [hot_rows(index_row(sender, t, step), 0, count), hot_rows(index_row(receiver, t, step), 0, count)],
                axis=0,
            )
            sums[...] += dot(hot, hg)

        piece(t, step, cot, grad_hbm, out_sem).start()
        return carry

    lax.fori_loop(0, steps, body, 0)
    for c in later:
        c.wait()
    direct[...] = (
        direct[...]
        + dot_nt(sums[:count, :].astype(BF), w1[width : 2 * width, :])
        + dot_nt(sums[count:, :].astype(BF), w1[2 * width :, :])
    )
    for c in fetch(last_sem, (direct, owned_hbm)):
        c.wait()
    for t in range(steps):
        piece(t, step, cot, grad_hbm, out_sem).wait()


def final_kernel(
    list_hbm, owned_hbm, n0, n1, n2, n3, n4, n5, far_hbm, out_hbm,
    slots, owned, returned, out, far_packed, far_wide, sems, last_sem,
):
    near = [(n, returned.at[pl.ds(i * NEAR, NEAR)]) for i, n in enumerate((n0, n1, n2, n3, n4, n5))]
    first = fetch(sems, (list_hbm, slots), *near, (far_hbm, far_packed), (owned_hbm, owned))
    first[0].wait()
    hot = hot_rows(slots[...], 0, owned.shape[0])
    for c in first[1:]:
        c.wait()
    unpack_far(far_packed, far_wide, returned)
    out[...] = (owned[...] + dot(hot, returned[...])).astype(BF)
    for c in fetch(last_sem, (out, out_hbm)):
        c.wait()


def kernel_call(body, outs, in_specs, out_specs, scratch, flops, moved):
    return pl.pallas_call(
        body,
        out_shape=outs,
        in_specs=in_specs,
        out_specs=out_specs,
        scratch_shapes=scratch,
        compiler_params=pltpu.CompilerParams(vmem_limit_bytes=VMEM_LIMIT),
        cost_estimate=pl.CostEstimate(flops=flops, bytes_accessed=moved, transcendentals=0),
    )


def on_device(
    nodes, edges, sender, receiver, tile_counts, send_list, edge_w1, edge_w2, edge_gain,
    node_w1, node_w2, node_gain, node_cotangent, edge_cotangent,
):
    count, width = nodes.shape
    slots = edges.shape[0]
    halo = send_list.shape[1]
    far_rows = halo - NEAR_TOTAL
    far_shape = (lax.axis_size(AXES), far_rows * width // 128 // lax.axis_size(AXES), 128)
    padded = -(-halo // 256) * 256
    v = pl.BlockSpec(memory_space=pltpu.VMEM)
    a = pl.BlockSpec(memory_space=pl.ANY)
    sds = jax.ShapeDtypeStruct
    sem = lambda n: pltpu.SemaphoreType.DMA((n,))
    near_shapes = [sds((NEAR, width), BF)] * 6 + [sds(far_shape, BF)]
    big = sds((slots, width), BF)
    far_packed = VMEM(far_shape, BF)
    far_wide = VMEM((far_rows * width // 128, 128), F32)
    wide = VMEM((slots, width), BF)
    lanes = VMEM((slots, 128), I16)
    index = VMEM((slots // 128, 128), jnp.int32)
    listed = VMEM((1, halo), jnp.int32)
    block = VMEM((count, width), BF)
    block32 = VMEM((count, width), F32)
    mat = VMEM((width, width), BF)
    vec = VMEM((1, width), F32)
    w1 = VMEM((3 * width, width), BF)
    square = 2 * count * width * width

    sender = sender.reshape(slots // 128, 128)
    receiver = receiver.reshape(slots // 128, 128)
    gain = edge_gain.reshape(1, width)
    ngain = node_gain.reshape(1, width)

    leaving = kernel_call(
        gather_kernel, near_shapes, [a, a], [v] * 7, [block, listed, far_wide, sem(2)],
        2 * halo * count * width, 2 * MIB,
    )(nodes, send_list)
    arrived = [shifted(leaving[i], near_offset(i)) for i in range(6)]
    far = exchange_far(leaving[6])

    n = slots // STEP_LOCAL
    part = kernel_call(
        local_kernel, big, [a] * 5, a,
        [block, index, index, w1, wide, wide, lanes, lanes, VMEM((2 * count, width), BF), VMEM((count + WINDOW + width, width), BF),
         pltpu.SMEM((slots // 128, 128), jnp.int32), sem(5), sem(n), sem(n)],
        square, MIB,
    )(nodes, sender, receiver, edge_w1, edges)

    n = slots // STEP_MAIN
    outs = kernel_call(
        main_kernel,
        [big, sds((count, width), BF), big] + near_shapes + [sds((count, width), F32)],
        [a] * 21,
        [a, a, a] + [v] * 7 + [a],
        [pltpu.SMEM(tile_counts.shape, jnp.int32), far_packed, far_wide,
         VMEM((halo, width), BF), index, index, mat, mat, vec, VMEM((2 * width, width), BF), mat, vec, block, block]
        + [wide] * 7
        + [lanes, lanes, VMEM((slots, 1), F32), VMEM((padded, width), BF), VMEM((padded, width), F32),
           block32, block, block, block32, mat, mat, VMEM((STEP_MAIN, width), BF)]
        + [sem(13), sem(5)] + [sem(n)] * 5 + [sem(2)],
        50 * square, 20 * MIB,
    )(
        tile_counts, *arrived, far, sender, receiver, edge_w1, edge_w2, gain, node_w1, node_w2, ngain,
        nodes, node_cotangent, part, edges, edge_cotangent,
    )
    edge_out, node_out, hgrad = outs[:3]
    back = outs[3:10]
    direct = outs[10]
    made = {i: shifted(back[k], -near_offset(i)) for k, i in enumerate(RETURN_ORDER)}
    returned = [made[i] for i in range(6)]
    far_back = exchange_far(back[6])

    n = slots // STEP_REST
    grad_edges, owned = kernel_call(
        rest_kernel, [big, sds((count, width), F32)], [a] * 6, [a, a],
        [index, index, w1, block32, wide, wide, VMEM((2 * count, width), F32), mat, pltpu.SMEM((slots // 128, 128), jnp.int32), sem(4), sem(2), sem(n), sem(n), sem(n), sem(1)],
        square, MIB,
    )(sender, receiver, edge_w1, direct, hgrad, edge_cotangent)

    grad_nodes = kernel_call(
        final_kernel, sds((count, width), BF), [a] * 9, a,
        [listed, block32, VMEM((halo, width), BF), block, far_packed, far_wide, sem(9), sem(1)], 2 * square, 3 * MIB,
    )(send_list, owned, *returned, far_back)
    return edge_out, node_out, grad_edges, grad_nodes


def solution(mesh):
    rows = P(AXES, None)
    flat = P(AXES)
    in_specs = (
        rows, rows, flat, flat, flat, rows, P(), P(), P(), P(), P(), P(), rows, rows,
    )
    return jax.shard_map(
        on_device, mesh=mesh, in_specs=in_specs, out_specs=(rows,) * 4, check_vma=False
    )
```
